32 devices in a mesh: groups: 2 (over y), batch: 4 (over z), pair: 2 (over x), sub: 2 (over core).
Axes of the slice: x: 2, y: 2, z: 4, core: 2. Of those that a mesh axis runs over, the one named last changes fastest.
Arguments:
- teacher_feats: bfloat16 [4096, 1024], P(('groups', 'batch', 'pair', 'sub')), parts along dimension 0, may hold values from -6 to 6
- student_feats: bfloat16 [4096, 384], P(('groups', 'batch', 'pair', 'sub')), parts along dimension 0, may hold values from -6 to 6
- head_weight: bfloat16 [384, 1024], replicated, may hold values from -0.3125 to 0.3125
- teacher_lse: float32 [4096], P(('groups', 'batch', 'pair', 'sub')), parts along dimension 0, may hold values from -1.5 to 1.5
- student_lse: float32 [4096], P(('groups', 'batch', 'pair', 'sub')), parts along dimension 0, may hold values from -1.5 to 1.5
Outputs:
- student_grad: bfloat16 [4096, 384], P(('groups', 'batch', 'pair', 'sub')), parts along dimension 0
- head_grad: float32 [768, 1024], P('groups'), parts along dimension 0
The draws below stay inside these ranges and needn't reach their ends.
There are 2 independent parts, one for each index of `groups`. The reference program is written for one: setup_inputs(seed, part) draws one part's arguments, and reference() takes and returns one part's arrays. A program takes and returns all parts, laid end to end along the dimension named above; an argument that names none is the same for every part. Nothing has to cross between parts.
All inputs are finite; a program needn't handle non-finite values.
Results may differ from the reference program's by a relative error of at most 0.011.
Values may be sent and summed in bfloat16 or wider, within the bound.
A program may use at most 64 MiB of HBM per device.

```python
import jax
import jax.numpy as jnp
from jax import lax

TD = 1024
SD = 384
ED = 1024
ROUNDS = 3
IMAGES = 2048
N_BATCH = 4


def block_levels(rng, shape, shards, smallest, top_value):
    level = 1.0
    for position, parts in shards:
        draws = jax.random.uniform(jax.random.fold_in(jax.random.fold_in(rng, 6), position), (parts,), jnp.float32, smallest / len(shards), top_value / len(shards))
        level = level * jnp.repeat(jnp.exp(draws), shape[position] // parts).reshape((-1,) + (1,) * (len(shape) - 1 - position))
    return level


def scatter_about(rng, shape, deviation, bound, pieces=(), kind=jnp.bfloat16):
    loudness = block_levels(rng, shape, pieces, -0.22, 0.18) if pieces else 1.0
    result = jax.random.normal(rng, shape, jnp.float32) * deviation * loudness
    return jnp.minimum(jnp.maximum(result, -bound), bound).astype(kind)


def setup_inputs(seed: int = 0, part: int = 0) -> dict:
    arg_keys = jax.random.split(jax.random.key(seed), 6)
    part_keys = jax.random.split(jax.random.fold_in(arg_keys[5], part), 6)
    return {
        "teacher_feats": scatter_about(part_keys[0], (IMAGES, TD), 1.0, 6.0, ((0, 16),)),
        "student_feats": scatter_about(part_keys[1], (IMAGES, SD), 1.0, 6.0, ((0, 16),)),
        "head_weight": scatter_about(arg_keys[2], (SD, ED), SD ** -0.5, 0.3125),
        "teacher_lse": jnp.clip(jax.random.uniform(part_keys[3], (IMAGES,), jnp.float32, -1.5, 1.5) * block_levels(part_keys[3], (IMAGES,), ((0, 16),), -0.4, 0.0), -1.5, 1.5),
        "student_lse": jnp.clip(jax.random.uniform(part_keys[4], (IMAGES,), jnp.float32, -1.5, 1.5) * block_levels(part_keys[4], (IMAGES,), ((0, 16),), -0.4, 0.0), -1.5, 1.5),
    }


TEACHER_TEMP = 0.04
STUDENT_TEMP = 0.05
LOSS_WEIGHT = 0.5
HEAD_SCALE = 0.0078125
EPSILON = 1e-06

def tile_grad(rows_t, rows_e, rows_s, cols_t, cols_e, cols_s):
    teacher_logits = lax.dot_general(rows_t, cols_t, (((1,), (1,)), ((), ())), preferred_element_type=jnp.float32) / TEACHER_TEMP
    student_logits = lax.dot_general(rows_e, cols_e, (((1,), (1,)), ((), ())), preferred_element_type=jnp.float32) / STUDENT_TEMP
    total = jnp.exp(student_logits - rows_s[:, 1:2]) - jnp.exp(teacher_logits - rows_s[:, 0:1])
    total = total + jnp.exp(student_logits - cols_s[None, :, 1]) - jnp.exp(teacher_logits - cols_s[None, :, 0])
    return (total * (LOSS_WEIGHT / STUDENT_TEMP)).astype(jnp.bfloat16)

def reference(teacher_feats, student_feats, head_weight, teacher_lse, student_lse):
    teacher_wide = teacher_feats.astype(jnp.float32)
    teacher_unit = (teacher_wide / jnp.sqrt(lax.optimization_barrier(jnp.sum(teacher_wide * teacher_wide, 1, keepdims=True)) + EPSILON)).astype(jnp.bfloat16)
    projected = jnp.dot(student_feats, head_weight, preferred_element_type=jnp.float32)
    magnitude = jnp.sqrt(lax.optimization_barrier(jnp.sum(projected * projected, 1, keepdims=True)) + EPSILON)
    unit = projected / magnitude
    unit_bf = unit.astype(jnp.bfloat16)
    stats = jnp.stack([teacher_lse, student_lse], 1)
    blocks = N_BATCH
    block_rows = teacher_feats.shape[0] // blocks

    def one_block(block_index, totals):
        start = (block_index * block_rows).astype(jnp.int32)
        rows_t = lax.dynamic_slice_in_dim(teacher_unit, start, block_rows, 0)
        rows_e = lax.dynamic_slice_in_dim(unit_bf, start, block_rows, 0)
        rows_s = lax.dynamic_slice_in_dim(stats, start, block_rows, 0)
        for offset in range(1, ROUNDS + 1):
            other = ((block_index + offset) % blocks * block_rows).astype(jnp.int32)
            cols_t = lax.dynamic_slice_in_dim(teacher_unit, other, block_rows, 0)
            cols_e = lax.dynamic_slice_in_dim(unit_bf, other, block_rows, 0)
            cols_s = lax.dynamic_slice_in_dim(stats, other, block_rows, 0)
            weights = tile_grad(rows_t, rows_e, rows_s, cols_t, cols_e, cols_s)
            row_part = jnp.dot(weights, cols_e, preferred_element_type=jnp.float32)
            col_part = lax.dot_general(weights, rows_e, (((0,), (0,)), ((), ())), preferred_element_type=jnp.float32)
            current = lax.dynamic_slice_in_dim(totals, start, block_rows, 0)
            totals = lax.dynamic_update_slice_in_dim(totals, current + row_part, start, 0)
            current = lax.dynamic_slice_in_dim(totals, other, block_rows, 0)
            totals = lax.dynamic_update_slice_in_dim(totals, current + col_part, other, 0)
        return totals
    embed_grad = lax.fori_loop(0, blocks, one_block, jnp.zeros(unit.shape, jnp.float32))
    along = lax.optimization_barrier(jnp.sum(unit * embed_grad, 1, keepdims=True))
    grad_proj = ((embed_grad - unit * along) / magnitude).astype(jnp.bfloat16)
    student_grad = lax.dot_general(grad_proj, head_weight, (((1,), (1,)), ((), ())), preferred_element_type=jnp.float32).astype(jnp.bfloat16)
    head_grad = lax.dot_general(student_feats, grad_proj, (((0,), (0,)), ((), ())), preferred_element_type=jnp.float32) * HEAD_SCALE
    return (student_grad, head_grad)
```

```python
import functools

import jax
import jax.numpy as jnp
from jax import lax
from jax.experimental import pallas as pl
from jax.experimental.pallas import tpu as pltpu
from jax.sharding import PartitionSpec as P

TEACHER_TEMP = 0.04
STUDENT_TEMP = 0.05
LOSS_WEIGHT = 0.5
HEAD_SCALE = 0.0078125
EPSILON = 1e-06
ROUNDS = 3
LANES = 128
CHUNKS = 2
STAT_ROWS = 16
MESH = pl.DeviceIdType.MESH
BF = jnp.bfloat16
F32 = jnp.float32


def nt(a, b):
    return lax.dot_general(a, b, (((1,), (1,)), ((), ())), preferred_element_type=F32)


def tn(a, b):
    return lax.dot_general(a, b, (((0,), (0,)), ((), ())), preferred_element_type=F32)


def project(feats, head):
    projected = jnp.dot(feats, head, preferred_element_type=F32)
    magnitude = jnp.sqrt(jnp.sum(projected * projected, 1, keepdims=True) + EPSILON)
    return projected / magnitude, magnitude


def kernel(
    n_batch, n_pair, tf_ref, sf_ref, hw_ref, tl_ref, sl_ref, sg_ref, head_ref,
    own, buf, t_own, u_own, unit_ref, acc, z_send, x_send, s_send, recv,
):
    rows, wide = tf_ref.shape
    sdim = sf_ref.shape[1]
    per = rows // CHUNKS
    t_tiles, s_tiles = wide // LANES, sdim // LANES
    stat_at = (t_tiles + s_tiles) * per
    hops = min(ROUNDS, n_batch - 1)
    ring = n_batch > 2 * ROUNDS
    times = 1.0 if ring else 2.0
    b, p, s = lax.axis_index("batch"), lax.axis_index("pair"), lax.axis_index("sub")

    def place(index):
        return lax.rem(index + n_batch, n_batch) if ring else index

    def when(index):
        if ring:
            return lambda f: f()
        return pl.when(jnp.logical_and(index >= 0, index < n_batch))

    barrier = pltpu.get_barrier_semaphore()
    for sign in (1, -1):
        @when(b + sign)
        def _():
            pl.semaphore_signal(
                barrier, inc=1, device_id={"batch": place(b + sign)}, device_id_type=MESH
            )
    for k in range(1, n_pair):
        pl.semaphore_signal(
            barrier, inc=1, device_id={"pair": lax.rem(p + k, n_pair)}, device_id_type=MESH
        )
    pl.semaphore_signal(barrier, inc=1, device_id={"sub": 1 - s}, device_id_type=MESH)

    wide_t = tf_ref[...].astype(F32)
    teacher = (
        wide_t / jnp.sqrt(jnp.sum(wide_t * wide_t, 1, keepdims=True) + EPSILON)
    ).astype(BF)
    t_own[...] = teacher
    stat_t, stat_s = jnp.exp(-tl_ref[...]), jnp.exp(-sl_ref[...])
    stat = jnp.concatenate([stat_t, stat_s, jnp.zeros((6, LANES), F32)], 0)
    high = stat.astype(BF)
    low = (stat - high.astype(F32)).astype(BF)
    stats = jnp.concatenate([high, low], 0)
    for q in range(CHUNKS):
        for k in range(t_tiles):
            own[q, k * per : (k + 1) * per, :] = teacher[
                q * per : (q + 1) * per, k * LANES : (k + 1) * LANES
            ]
        for k in range(s_tiles):
            at = (t_tiles + k) * per
            own[q, at : at + per, :] = sf_ref[
                q * per : (q + 1) * per, k * LANES : (k + 1) * LANES
            ]
        own[q, stat_at : stat_at + STAT_ROWS, :] = stats

    peers = n_pair + 2
    if not ring:
        peers = n_pair + jnp.minimum(b, 1) + jnp.minimum(n_batch - 1 - b, 1)
    pl.semaphore_wait(barrier, peers)

    def z_copy(d, h, q, src):
        return pltpu.make_async_remote_copy(
            src_ref=src,
            dst_ref=buf.at[d, h, p, s, q],
            send_sem=z_send.at[d, h, q],
            recv_sem=recv.at[d, h, p, s, q],
            device_id={"batch": place(b + 1 - 2 * d)},
            device_id_type=MESH,
        )

    def x_copy(d, h, q, k):
        return pltpu.make_async_remote_copy(
            src_ref=buf.at[d, h, p, s, q],
            dst_ref=buf.at[d, h, p, s, q],
            send_sem=x_send.at[d, h, k, q],
            recv_sem=recv.at[d, h, p, s, q],
            device_id={"pair": lax.rem(p + k, n_pair)},
            device_id_type=MESH,
        )

    def s_copy(d, h, q, source):
        return pltpu.make_async_remote_copy(
            src_ref=buf.at[d, h, source, s, q],
            dst_ref=buf.at[d, h, source, s, q],
            send_sem=s_send.at[d, h, source, q],
            recv_sem=recv.at[d, h, source, s, q],
            device_id={"sub": 1 - s},
            device_id_type=MESH,
        )

    def arrived(d, h, source, core, q):
        pltpu.make_async_remote_copy(
            src_ref=buf.at[d, h, source, core, q],
            dst_ref=buf.at[d, h, source, core, q],
            send_sem=s_send.at[d, h, source, q],
            recv_sem=recv.at[d, h, source, core, q],
            device_id={"sub": 1 - s},
            device_id_type=MESH,
        ).wait_recv()

    for q in range(CHUNKS):
        for d in range(2):
            @when(b + 1 - 2 * d)
            def _():
                z_copy(d, 0, q, own.at[q]).start()

    unit, magnitude = project(sf_ref[...], hw_ref[...])
    unit_ref[...] = unit
    u_own[...] = unit.astype(BF)
    acc[...] = jnp.zeros_like(acc)
    tall = stat.T
    row_t, row_s = tall[:, 0:1], tall[:, 1:2]

    def source_of(d, h):
        return b - (1 - 2 * d) * (h + 1)

    def z_step(h, q):
        def each(d, carry):
            @when(source_of(d, h))
            def _():
                arrived(d, h, p, s, q)

                @pl.when(h < hops - 1)
                def _():
                    @when(b + 1 - 2 * d)
                    def _():
                        z_copy(d, h + 1, q, buf.at[d, h, p, s, q]).start()

                for k in range(1, n_pair):
                    x_copy(d, h, q, k).start()
                s_copy(d, h, q, p).start()
            return carry

        lax.fori_loop(0, 2, each, 0)

    def x_step(h, q):
        def each(d, carry):
            @when(source_of(d, h))
            def _():
                for k in range(1, n_pair):
                    source = lax.rem(p + k, n_pair)
                    arrived(d, h, source, s, q)
                    s_copy(d, h, q, source).start()
            return carry

        lax.fori_loop(0, 2, each, 0)

    def tile(d, h, source):
        for q in range(CHUNKS):
            arrived(d, h, source, 1 - s, q)
        t_parts, f_parts, st = [], [], []
        for core in range(2):
            for q in range(CHUNKS):
                t_parts.append(jnp.concatenate(
                    [buf[d, h, source, core, q, k * per : (k + 1) * per, :] for k in range(t_tiles)], 1
                ))
                f_parts.append(jnp.concatenate(
                    [
                        buf[d, h, source, core, q, (t_tiles + k) * per : (t_tiles + k + 1) * per, :]
                        for k in range(s_tiles)
                    ], 1
                ))
            raw = buf[d, h, source, core, 0, stat_at : stat_at + STAT_ROWS, :].astype(F32)
            st.append(raw[0:8] + raw[8:16])
        cols_t = jnp.concatenate(t_parts, 0)
        cols_f = jnp.concatenate(f_parts, 0)
        cols_s = jnp.concatenate(st, 1)
        cols_u = project(cols_f, hw_ref[...])[0].astype(BF)
        zt = nt(t_own[...], cols_t) * (1.0 / TEACHER_TEMP)
        zs = nt(u_own[...], cols_u) * (1.0 / STUDENT_TEMP)
        g = jnp.exp(zs) * (row_s + cols_s[1:2]) - jnp.exp(zt) * (row_t + cols_s[0:1])
        weights = (g * (LOSS_WEIGHT / STUDENT_TEMP)).astype(BF)
        acc[...] += jnp.dot(weights, cols_u, preferred_element_type=F32)

    def work(h, first, last):
        def each(d, carry):
            @when(source_of(d, h))
            def _():
                def one(k, c):
                    tile(d, h, lax.rem(p + k, n_pair))
                    return c

                lax.fori_loop(first, last, one, 0)
            return carry

        lax.fori_loop(0, 2, each, 0)

    def stage(h, carry):
        for q in range(CHUNKS):
            @pl.when(h < hops)
            def _():
                z_step(h, q)

            if q == 0:
                @pl.when(h > 0)
                def _():
                    x_step(h - 1, CHUNKS - 1)
                    work(h - 1, 0, n_pair)
            else:
                @pl.when(h < hops)
                def _():
                    x_step(h, q - 1)
        return carry

    lax.fori_loop(0, hops + 1, stage, 0)

    embed = acc[...] * times
    unit = unit_ref[...]
    along = jnp.sum(unit * embed, 1, keepdims=True)
    grad_proj = ((embed - unit * along) / magnitude).astype(BF)
    sg_ref[...] = nt(grad_proj, hw_ref[...]).astype(BF)
    head_ref[...] = tn(sf_ref[...], grad_proj)

    for d in range(2):
        @when(b + 1 - 2 * d)
        def _():
            for q in range(CHUNKS):
                z_copy(d, 0, q, own.at[q]).wait_send()
        for h in range(hops):
            @when(source_of(d, h))
            def _():
                for q in range(CHUNKS):
                    if h < hops - 1:
                        @when(b + 1 - 2 * d)
                        def _():
                            z_copy(d, h + 1, q, buf.at[d, h, p, s, q]).wait_send()
                    for k in range(1, n_pair):
                        x_copy(d, h, q, k).wait_send()
                    for k in range(n_pair):
                        s_copy(d, h, q, lax.rem(p + k, n_pair)).wait_send()


def solution(mesh):
    n_batch, n_pair = mesh.shape["batch"], mesh.shape["pair"]
    hops = min(ROUNDS, n_batch - 1)

    def body(teacher_feats, student_feats, head_weight, teacher_lse, student_lse):
        rows, wide = teacher_feats.shape
        sdim, edim = head_weight.shape
        depth = (wide + sdim) // LANES * (rows // CHUNKS) + STAT_ROWS
        vmem = pl.BlockSpec(memory_space=pltpu.VMEM)
        student_grad, local_head = pl.pallas_call(
            functools.partial(kernel, n_batch, n_pair),
            out_shape=(
                jax.ShapeDtypeStruct((rows, sdim), BF),
                jax.ShapeDtypeStruct((sdim, edim), F32),
            ),
            in_specs=[vmem] * 5,
            out_specs=(vmem, vmem),
            scratch_shapes=[
                pltpu.VMEM((CHUNKS, depth, LANES), BF),
                pltpu.VMEM((2, hops, n_pair, 2, CHUNKS, depth, LANES), BF),
                pltpu.VMEM((rows, wide), BF),
                pltpu.VMEM((rows, edim), BF),
                pltpu.VMEM((rows, edim), F32),
                pltpu.VMEM((rows, edim), F32),
                pltpu.SemaphoreType.DMA((2, hops, CHUNKS)),
                pltpu.SemaphoreType.DMA((2, hops, n_pair, CHUNKS)),
                pltpu.SemaphoreType.DMA((2, hops, n_pair, CHUNKS)),
                pltpu.SemaphoreType.DMA((2, hops, n_pair, 2, CHUNKS)),
            ],
            compiler_params=pltpu.CompilerParams(
                collective_id=0, has_side_effects=True, vmem_limit_bytes=56 * 1024 * 1024
            ),
        )(
            teacher_feats, student_feats, head_weight,
            teacher_lse.reshape(1, rows), student_lse.reshape(1, rows),
        )
        head_grad = lax.psum(local_head, ("batch", "pair", "sub")) * HEAD_SCALE
        return student_grad, head_grad

    in_specs = (
        P(("groups", "batch", "pair", "sub"), None),
        P(("groups", "batch", "pair", "sub"), None),
        P(),
        P(("groups", "batch", "pair", "sub")),
        P(("groups", "batch", "pair", "sub")),
    )
    out_specs = (P(("groups", "batch", "pair", "sub"), None), P("groups", None))
    return jax.shard_map(body, mesh=mesh, in_specs=in_specs, out_specs=out_specs, check_vma=False)
```

```python
import functools

import jax
import jax.numpy as jnp
from jax import lax
from jax.experimental import pallas as pl
from jax.experimental.pallas import tpu as pltpu
from jax.sharding import PartitionSpec as P

TEACHER_TEMP = 0.04
STUDENT_TEMP = 0.05
LOSS_WEIGHT = 0.5
HEAD_SCALE = 0.0078125
EPSILON = 1e-06
ROUNDS = 3
LANES = 128
CHUNKS = 2
STAT_ROWS = 16
MESH = pl.DeviceIdType.MESH
BF = jnp.bfloat16
F32 = jnp.float32


def nt(a, b):
    return lax.dot_general(a, b, (((1,), (1,)), ((), ())), preferred_element_type=F32)


def tn(a, b):
    return lax.dot_general(a, b, (((0,), (0,)), ((), ())), preferred_element_type=F32)


def project(feats, head):
    projected = jnp.dot(feats, head, preferred_element_type=F32)
    magnitude = jnp.sqrt(jnp.sum(projected * projected, 1, keepdims=True) + EPSILON)
    return projected / magnitude, magnitude


def kernel(
    n_batch, n_pair, tf_ref, sf_ref, hw_ref, tl_ref, sl_ref, sg_ref, head_ref,
    own, buf, t_own, u_own, unit_ref, acc, part, half_out, half_in, mine, chunks, sums,
    z_send, x_send, s_send, recv,
    half_send, half_recv, c_send, c_recv, b_send, b_recv, f_send,
):
    rows, wide = tf_ref.shape
    sdim = sf_ref.shape[1]
    per = rows // CHUNKS
    t_tiles, s_tiles = wide // LANES, sdim // LANES
    stat_at = (t_tiles + s_tiles) * per
    hops = min(ROUNDS, n_batch - 1)
    ring = n_batch > 2 * ROUNDS
    times = 1.0 if ring else 2.0
    b, p, s = lax.axis_index("batch"), lax.axis_index("pair"), lax.axis_index("sub")

    def place(index):
        return lax.rem(index + n_batch, n_batch) if ring else index

    def when(index):
        if ring:
            return lambda f: f()
        return pl.when(jnp.logical_and(index >= 0, index < n_batch))

    chips = n_batch * n_pair
    chip = b * n_pair + p
    tiles, half, _ = half_out.shape
    piece = chunks.shape[1]
    owners = sums.shape[1]

    def at_chip(index):
        return {"batch": index // n_pair, "pair": lax.rem(index, n_pair)}

    def owns(index):
        return pl.when(index < owners) if owners < chips else lambda f: f()

    def others(f):
        def one(k, carry):
            f(lax.rem(chip + k, chips))
            return carry

        lax.fori_loop(1, chips, one, 0)

    barrier = pltpu.get_barrier_semaphore()

    def greet(other):
        pl.semaphore_signal(barrier, inc=1, device_id=at_chip(other), device_id_type=MESH)

    others(greet)
    pl.semaphore_signal(barrier, inc=1, device_id={"sub": 1 - s}, device_id_type=MESH)

    wide_t = tf_ref[...].astype(F32)
    teacher = (
        wide_t / jnp.sqrt(jnp.sum(wide_t * wide_t, 1, keepdims=True) + EPSILON)
    ).astype(BF)
    t_own[...] = teacher
    stat_t, stat_s = jnp.exp(-tl_ref[...]), jnp.exp(-sl_ref[...])
    stat = jnp.concatenate([stat_t, stat_s, jnp.zeros((6, LANES), F32)], 0)
    high = stat.astype(BF)
    low = (stat - high.astype(F32)).astype(BF)
    stats = jnp.concatenate([high, low], 0)
    for q in range(CHUNKS):
        for k in range(t_tiles):
            own[q, k * per : (k + 1) * per, :] = teacher[
                q * per : (q + 1) * per, k * LANES : (k + 1) * LANES
            ]
        for k in range(s_tiles):
            at = (t_tiles + k) * per
            own[q, at : at + per, :] = sf_ref[
                q * per : (q + 1) * per, k * LANES : (k + 1) * LANES
            ]
        own[q, stat_at : stat_at + STAT_ROWS, :] = stats

    pl.semaphore_wait(barrier, chips)

    def z_copy(d, h, q, src):
        return pltpu.make_async_remote_copy(
            src_ref=src,
            dst_ref=buf.at[d, h, p, s, q],
            send_sem=z_send.at[d, h, q],
            recv_sem=recv.at[d, h, p, s, q],
            device_id={"batch": place(b + 1 - 2 * d)},
            device_id_type=MESH,
        )

    def x_copy(d, h, q, k):
        return pltpu.make_async_remote_copy(
            src_ref=buf.at[d, h, p, s, q],
            dst_ref=buf.at[d, h, p, s, q],
            send_sem=x_send.at[d, h, k, q],
            recv_sem=recv.at[d, h, p, s, q],
            device_id={"pair": lax.rem(p + k, n_pair)},
            device_id_type=MESH,
        )

    def s_copy(d, h, q, source):
        return pltpu.make_async_remote_copy(
            src_ref=buf.at[d, h, source, s, q],
            dst_ref=buf.at[d, h, source, s, q],
            send_sem=s_send.at[d, h, source, q],
            recv_sem=recv.at[d, h, source, s, q],
            device_id={"sub": 1 - s},
            device_id_type=MESH,
        )

    def arrived(d, h, source, core, q):
        pltpu.make_async_remote_copy(
            src_ref=buf.at[d, h, source, core, q],
            dst_ref=buf.at[d, h, source, core, q],
            send_sem=s_send.at[d, h, source, q],
            recv_sem=recv.at[d, h, source, core, q],
            device_id={"sub": 1 - s},
            device_id_type=MESH,
        ).wait_recv()

    for q in range(CHUNKS):
        for d in range(2):
            @when(b + 1 - 2 * d)
            def _():
                z_copy(d, 0, q, own.at[q]).start()

    unit, magnitude = project(sf_ref[...], hw_ref[...])
    unit_ref[...] = unit
    u_own[...] = unit.astype(BF)
    acc[...] = jnp.zeros_like(acc)
    tall = stat.T
    row_t, row_s = tall[:, 0:1], tall[:, 1:2]

    def source_of(d, h):
        return b - (1 - 2 * d) * (h + 1)

    def z_step(h, q):
        def each(d, carry):
            @when(source_of(d, h))
            def _():
                arrived(d, h, p, s, q)

                @pl.when(h < hops - 1)
                def _():
                    @when(b + 1 - 2 * d)
                    def _():
                        z_copy(d, h + 1, q, buf.at[d, h, p, s, q]).start()

                for k in range(1, n_pair):
                    x_copy(d, h, q, k).start()
                s_copy(d, h, q, p).start()
            return carry

        lax.fori_loop(0, 2, each, 0)

    def x_step(h, q):
        def each(d, carry):
            @when(source_of(d, h))
            def _():
                for k in range(1, n_pair):
                    source = lax.rem(p + k, n_pair)
                    arrived(d, h, source, s, q)
                    s_copy(d, h, q, source).start()
            return carry

        lax.fori_loop(0, 2, each, 0)

    def tile(d, h, source):
        for q in range(CHUNKS):
            arrived(d, h, source, 1 - s, q)
        t_parts, f_parts, st = [], [], []
        for core in range(2):
            for q in range(CHUNKS):
                t_parts.append(jnp.concatenate(
                    [buf[d, h, source, core, q, k * per : (k + 1) * per, :] for k in range(t_tiles)], 1
                ))
                f_parts.append(jnp.concatenate(
                    [
                        buf[d, h, source, core, q, (t_tiles + k) * per : (t_tiles + k + 1) * per, :]
                        for k in range(s_tiles)
                    ], 1
                ))
            raw = buf[d, h, source, core, 0, stat_at : stat_at + STAT_ROWS, :].astype(F32)
            st.append(raw[0:8] + raw[8:16])
        cols_t = jnp.concatenate(t_parts, 0)
        cols_f = jnp.concatenate(f_parts, 0)
        cols_s = jnp.concatenate(st, 1)
        cols_u = project(cols_f, hw_ref[...])[0].astype(BF)
        zt = nt(t_own[...], cols_t) * (1.0 / TEACHER_TEMP)
        zs = nt(u_own[...], cols_u) * (1.0 / STUDENT_TEMP)
        g = jnp.exp(zs) * (row_s + cols_s[1:2]) - jnp.exp(zt) * (row_t + cols_s[0:1])
        weights = (g * (LOSS_WEIGHT / STUDENT_TEMP)).astype(BF)
        acc[...] += jnp.dot(weights, cols_u, preferred_element_type=F32)

    def work(h, first, last):
        def each(d, carry):
            @when(source_of(d, h))
            def _():
                def one(k, c):
                    tile(d, h, lax.rem(p + k, n_pair))
                    return c

                lax.fori_loop(first, last, one, 0)
            return carry

        lax.fori_loop(0, 2, each, 0)

    def stage(h, carry):
        for q in range(CHUNKS):
            @pl.when(h < hops)
            def _():
                z_step(h, q)

            if q == 0:
                @pl.when(h > 0)
                def _():
                    x_step(h - 1, CHUNKS - 1)
                    work(h - 1, 0, n_pair)
            else:
                @pl.when(h < hops)
                def _():
                    x_step(h, q - 1)
        return carry

    lax.fori_loop(0, hops + 1, stage, 0)

    embed = acc[...] * times
    unit = unit_ref[...]
    along = jnp.sum(unit * embed, 1, keepdims=True)
    grad_proj = ((embed - unit * along) / magnitude).astype(BF)
    local = tn(sf_ref[...], grad_proj)
    for k in range(tiles):
        part[k] = local[:, k * LANES : (k + 1) * LANES]

    here = pl.ds(pl.multiple_of(s * half, STAT_ROWS), half)
    there = pl.ds(pl.multiple_of((1 - s) * half, STAT_ROWS), half)
    half_out[...] = part[:, there, :].astype(BF)
    swap = pltpu.make_async_remote_copy(
        src_ref=half_out, dst_ref=half_in, send_sem=half_send.at[0], recv_sem=half_recv.at[0],
        device_id={"sub": 1 - s}, device_id_type=MESH,
    )
    swap.start()
    sg_ref[...] = nt(grad_proj, hw_ref[...]).astype(BF)
    swap.wait()
    part[:, here, :] = part[:, here, :] + half_in[...].astype(F32)
    mine[...] = part[:, here, :].astype(BF)

    def piece_of(index):
        return lax.rem(index, tiles), index // tiles * piece

    def c_copy(owner, source):
        tile_at, row_at = piece_of(owner)
        return pltpu.make_async_remote_copy(
            src_ref=mine.at[tile_at, pl.ds(pl.multiple_of(row_at, STAT_ROWS), piece)],
            dst_ref=chunks.at[source],
            send_sem=c_send.at[owner], recv_sem=c_recv.at[source],
            device_id=at_chip(owner), device_id_type=MESH,
        )

    def b_copy(other, source):
        return pltpu.make_async_remote_copy(
            src_ref=sums.at[s, source], dst_ref=sums.at[s, source],
            send_sem=b_send.at[other], recv_sem=b_recv.at[s, source],
            device_id=at_chip(other), device_id_type=MESH,
        )

    def f_copy(source, core):
        return pltpu.make_async_remote_copy(
            src_ref=sums.at[core, source], dst_ref=sums.at[core, source],
            send_sem=f_send.at[source], recv_sem=b_recv.at[core, source],
            device_id={"sub": 1 - s}, device_id_type=MESH,
        )

    def scatter(owner):
        @owns(owner)
        def _():
            c_copy(owner, chip).start()

    others(scatter)

    @owns(chip)
    def _():
        tile_at, row_at = piece_of(chip)
        first = part[tile_at, pl.ds(pl.multiple_of(s * half + row_at, STAT_ROWS), piece), :]

        def add(k, total):
            source = lax.rem(chip + k, chips)
            c_copy(chip, source).wait_recv()
            return total + chunks[source].astype(F32)

        sums[s, chip] = lax.fori_loop(1, chips, add, first).astype(BF)
        others(lambda other: b_copy(other, chip).start())
        f_copy(chip, s).start()

    def pass_on(source):
        @owns(source)
        def _():
            b_copy(source, source).wait_recv()
            f_copy(source, s).start()

    others(pass_on)

    def place_piece(core, source):
        tile_at, row_at = source % tiles, source // tiles * piece
        head_ref[
            core * half + row_at : core * half + row_at + piece,
            tile_at * LANES : (tile_at + 1) * LANES,
        ] = sums[core, source]

    for source in range(owners):
        f_copy(source, 1 - s).wait_recv()
    for source in range(owners):
        for core in range(2):
            place_piece(core, source)

    def left(other):
        @owns(other)
        def _():
            c_copy(other, chip).wait_send()

        @owns(chip)
        def _():
            b_copy(other, chip).wait_send()

    others(left)
    for source in range(owners):
        f_copy(source, s).wait_send()

    for d in range(2):
        @when(b + 1 - 2 * d)
        def _():
            for q in range(CHUNKS):
                z_copy(d, 0, q, own.at[q]).wait_send()
        for h in range(hops):
            @when(source_of(d, h))
            def _():
                for q in range(CHUNKS):
                    if h < hops - 1:
                        @when(b + 1 - 2 * d)
                        def _():
                            z_copy(d, h + 1, q, buf.at[d, h, p, s, q]).wait_send()
                    for k in range(1, n_pair):
                        x_copy(d, h, q, k).wait_send()
                    for k in range(n_pair):
                        s_copy(d, h, q, lax.rem(p + k, n_pair)).wait_send()


def solution(mesh):
    n_batch, n_pair = mesh.shape["batch"], mesh.shape["pair"]
    hops = min(ROUNDS, n_batch - 1)

    def body(teacher_feats, student_feats, head_weight, teacher_lse, student_lse):
        rows, wide = teacher_feats.shape
        sdim, edim = head_weight.shape
        depth = (wide + sdim) // LANES * (rows // CHUNKS) + STAT_ROWS
        chips, tiles, half = n_batch * n_pair, edim // LANES, sdim // 2
        piece = min(
            size for size in range(STAT_ROWS, half + 1, STAT_ROWS)
            if half % size == 0 and half // size * tiles <= chips
        )
        owners = half // piece * tiles
        vmem = pl.BlockSpec(memory_space=pltpu.VMEM)
        student_grad, head_sum = pl.pallas_call(
            functools.partial(kernel, n_batch, n_pair),
            out_shape=(
                jax.ShapeDtypeStruct((rows, sdim), BF),
                jax.ShapeDtypeStruct((sdim, edim), BF),
            ),
            in_specs=[vmem] * 5,
            out_specs=(vmem, vmem),
            scratch_shapes=[
                pltpu.VMEM((CHUNKS, depth, LANES), BF),
                pltpu.VMEM((2, hops, n_pair, 2, CHUNKS, depth, LANES), BF),
                pltpu.VMEM((rows, wide), BF),
                pltpu.VMEM((rows, edim), BF),
                pltpu.VMEM((rows, edim), F32),
                pltpu.VMEM((rows, edim), F32),
                pltpu.VMEM((tiles, sdim, LANES), F32),
                pltpu.VMEM((tiles, half, LANES), BF),
                pltpu.VMEM((tiles, half, LANES), BF),
                pltpu.VMEM((tiles, half, LANES), BF),
                pltpu.VMEM((chips, piece, LANES), BF),
                pltpu.VMEM((2, owners, piece, LANES), BF),
                pltpu.SemaphoreType.DMA((2, hops, CHUNKS)),
                pltpu.SemaphoreType.DMA((2, hops, n_pair, CHUNKS)),
                pltpu.SemaphoreType.DMA((2, hops, n_pair, CHUNKS)),
                pltpu.SemaphoreType.DMA((2, hops, n_pair, 2, CHUNKS)),
                pltpu.SemaphoreType.DMA((1,)),
                pltpu.SemaphoreType.DMA((1,)),
                pltpu.SemaphoreType.DMA((chips,)),
                pltpu.SemaphoreType.DMA((chips,)),
                pltpu.SemaphoreType.DMA((chips,)),
                pltpu.SemaphoreType.DMA((2, owners)),
                pltpu.SemaphoreType.DMA((owners,)),
            ],
            compiler_params=pltpu.CompilerParams(
                collective_id=0, has_side_effects=True, vmem_limit_bytes=56 * 1024 * 1024
            ),
        )(
            teacher_feats, student_feats, head_weight,
            teacher_lse.reshape(1, rows), student_lse.reshape(1, rows),
        )
        head_grad = head_sum.astype(F32) * HEAD_SCALE
        return student_grad, head_grad

    in_specs = (
        P(("groups", "batch", "pair", "sub"), None),
        P(("groups", "batch", "pair", "sub"), None),
        P(),
        P(("groups", "batch", "pair", "sub")),
        P(("groups", "batch", "pair", "sub")),
    )
    out_specs = (P(("groups", "batch", "pair", "sub"), None), P("groups", None))
    return jax.shard_map(body, mesh=mesh, in_specs=in_specs, out_specs=out_specs, check_vma=False)
```

```python
import functools

import jax
import jax.numpy as jnp
from jax import lax
from jax.experimental import pallas as pl
from jax.experimental.pallas import tpu as pltpu
from jax.sharding import PartitionSpec as P

TEACHER_TEMP = 0.04
STUDENT_TEMP = 0.05
LOSS_WEIGHT = 0.5
HEAD_SCALE = 0.0078125
EPSILON = 1e-06
ROUNDS = 3
LANES = 128
CHUNKS = 2
STAT_ROWS = 16
MESH = pl.DeviceIdType.MESH
BF = jnp.bfloat16
F32 = jnp.float32


def nt(a, b):
    return lax.dot_general(a, b, (((1,), (1,)), ((), ())), preferred_element_type=F32)


def tn(a, b):
    return lax.dot_general(a, b, (((0,), (0,)), ((), ())), preferred_element_type=F32)


def project(feats, head):
    projected = jnp.dot(feats, head, preferred_element_type=F32)
    magnitude = jnp.sqrt(jnp.sum(projected * projected, 1, keepdims=True) + EPSILON)
    return projected / magnitude, magnitude


def kernel(
    n_batch, n_pair, tf_ref, sf_ref, hw_ref, tl_ref, sl_ref, sg_ref, head_ref,
    own, buf, t_own, u_own, unit_ref, acc, part, half_out, half_in, mine, chunks, sums,
    z_send, x_send, s_send, recv,
    half_send, half_recv, c_send, c_recv, b_send, b_recv, f_send,
):
    rows, wide = tf_ref.shape
    sdim = sf_ref.shape[1]
    per = rows // CHUNKS
    t_tiles, s_tiles = wide // LANES, sdim // LANES
    stat_at = (t_tiles + s_tiles) * per
    hops = min(ROUNDS, n_batch - 1)
    ring = n_batch > 2 * ROUNDS
    times = 1.0 if ring else 2.0
    b, p, s = lax.axis_index("batch"), lax.axis_index("pair"), lax.axis_index("sub")

    def place(index):
        return lax.rem(index + n_batch, n_batch) if ring else index

    def when(index):
        if ring:
            return lambda f: f()
        return pl.when(jnp.logical_and(index >= 0, index < n_batch))

    chips = n_batch * n_pair
    chip = b * n_pair + p
    tiles, half, _ = half_out.shape
    piece = chunks.shape[1]
    owners = sums.shape[1]

    def at_chip(index):
        return {"batch": index // n_pair, "pair": lax.rem(index, n_pair)}

    def owns(index):
        return pl.when(index < owners) if owners < chips else lambda f: f()

    def others(f):
        def one(k, carry):
            f(lax.rem(chip + k, chips))
            return carry

        lax.fori_loop(1, chips, one, 0)

    barrier = pltpu.get_barrier_semaphore()

    def greet(other):
        pl.semaphore_signal(barrier, inc=1, device_id=at_chip(other), device_id_type=MESH)

    others(greet)
    pl.semaphore_signal(barrier, inc=1, device_id={"sub": 1 - s}, device_id_type=MESH)

    wide_t = tf_ref[...].astype(F32)
    teacher = (
        wide_t / jnp.sqrt(jnp.sum(wide_t * wide_t, 1, keepdims=True) + EPSILON)
    ).astype(BF)
    t_own[...] = teacher
    stat_t, stat_s = jnp.exp(-tl_ref[...]), jnp.exp(-sl_ref[...])
    stat = jnp.concatenate([stat_t, stat_s, jnp.zeros((6, LANES), F32)], 0)
    high = stat.astype(BF)
    low = (stat - high.astype(F32)).astype(BF)
    stats = jnp.concatenate([high, low], 0)
    for q in range(CHUNKS):
        for k in range(t_tiles):
            own[q, k * per : (k + 1) * per, :] = teacher[
                q * per : (q + 1) * per, k * LANES : (k + 1) * LANES
            ]
        for k in range(s_tiles):
            at = (t_tiles + k) * per
            own[q, at : at + per, :] = sf_ref[
                q * per : (q + 1) * per, k * LANES : (k + 1) * LANES
            ]
        own[q, stat_at : stat_at + STAT_ROWS, :] = stats

    pl.semaphore_wait(barrier, chips)

    def z_copy(d, h, q, src):
        return pltpu.make_async_remote_copy(
            src_ref=src,
            dst_ref=buf.at[d, h, p, s, q],
            send_sem=z_send.at[d, h, q],
            recv_sem=recv.at[d, h, p, s, q],
            device_id={"batch": place(b + 1 - 2 * d)},
            device_id_type=MESH,
        )

    def x_copy(d, h, q, k):
        return pltpu.make_async_remote_copy(
            src_ref=buf.at[d, h, p, s, q],
            dst_ref=buf.at[d, h, p, s, q],
            send_sem=x_send.at[d, h, k, q],
            recv_sem=recv.at[d, h, p, s, q],
            device_id={"pair": lax.rem(p + k, n_pair)},
            device_id_type=MESH,
        )

    def s_copy(d, h, q, source):
        return pltpu.make_async_remote_copy(
            src_ref=buf.at[d, h, source, s, q],
            dst_ref=buf.at[d, h, source, s, q],
            send_sem=s_send.at[d, h, source, q],
            recv_sem=recv.at[d, h, source, s, q],
            device_id={"sub": 1 - s},
            device_id_type=MESH,
        )

    def arrived(d, h, source, core, q):
        pltpu.make_async_remote_copy(
            src_ref=buf.at[d, h, source, core, q],
            dst_ref=buf.at[d, h, source, core, q],
            send_sem=s_send.at[d, h, source, q],
            recv_sem=recv.at[d, h, source, core, q],
            device_id={"sub": 1 - s},
            device_id_type=MESH,
        ).wait_recv()

    for q in range(CHUNKS):
        for d in range(2):
            @when(b + 1 - 2 * d)
            def _():
                z_copy(d, 0, q, own.at[q]).start()

    unit, magnitude = project(sf_ref[...], hw_ref[...])
    unit_ref[...] = unit
    u_own[...] = unit.astype(BF)
    acc[...] = jnp.zeros_like(acc)
    tall = stat.T
    row_t, row_s = tall[:, 0:1], tall[:, 1:2]

    def source_of(d, h):
        return b - (1 - 2 * d) * (h + 1)

    def z_step(h, q):
        def each(d, carry):
            @when(source_of(d, h))
            def _():
                arrived(d, h, p, s, q)

                @pl.when(h < hops - 1)
                def _():
                    @when(b + 1 - 2 * d)
                    def _():
                        z_copy(d, h + 1, q, buf.at[d, h, p, s, q]).start()

                for k in range(1, n_pair):
                    x_copy(d, h, q, k).start()
                s_copy(d, h, q, p).start()
            return carry

        lax.fori_loop(0, 2, each, 0)

    def x_step(h, q):
        def each(d, carry):
            @when(source_of(d, h))
            def _():
                for k in range(1, n_pair):
                    source = lax.rem(p + k, n_pair)
                    arrived(d, h, source, s, q)
                    s_copy(d, h, q, source).start()
            return carry

        lax.fori_loop(0, 2, each, 0)

    def tile(d, h, source):
        for q in range(CHUNKS):
            arrived(d, h, source, 1 - s, q)
        t_parts, f_parts, st = [], [], []
        for core in range(2):
            for q in range(CHUNKS):
                t_parts.append(jnp.concatenate(
                    [buf[d, h, source, core, q, k * per : (k + 1) * per, :] for k in range(t_tiles)], 1
                ))
                f_parts.append(jnp.concatenate(
                    [
                        buf[d, h, source, core, q, (t_tiles + k) * per : (t_tiles + k + 1) * per, :]
                        for k in range(s_tiles)
                    ], 1
                ))
            raw = buf[d, h, source, core, 0, stat_at : stat_at + STAT_ROWS, :].astype(F32)
            st.append(raw[0:8] + raw[8:16])
        cols_t = jnp.concatenate(t_parts, 0)
        cols_f = jnp.concatenate(f_parts, 0)
        cols_s = jnp.concatenate(st, 1)
        cols_u = project(cols_f, hw_ref[...])[0].astype(BF)
        zt = nt(t_own[...], cols_t) * (1.0 / TEACHER_TEMP)
        zs = nt(u_own[...], cols_u) * (1.0 / STUDENT_TEMP)
        g = jnp.exp(zs) * (row_s + cols_s[1:2]) - jnp.exp(zt) * (row_t + cols_s[0:1])
        weights = (g * (LOSS_WEIGHT / STUDENT_TEMP)).astype(BF)
        acc[...] += jnp.dot(weights, cols_u, preferred_element_type=F32)

    def work(h, first, last):
        def each(d, carry):
            @when(source_of(d, h))
            def _():
                def one(k, c):
                    tile(d, h, lax.rem(p + k, n_pair))
                    return c

                lax.fori_loop(first, last, one, 0)
            return carry

        lax.fori_loop(0, 2, each, 0)

    def stage(h, carry):
        for q in range(CHUNKS):
            @pl.when(h < hops)
            def _():
                z_step(h, q)

            if q > 0:
                @pl.when(h < hops)
                def _():
                    x_step(h, q - 1)

            @pl.when(h > 0)
            def _():
                if q == 0:
                    @pl.when(h == hops)
                    def _():
                        work(h - 1, 0, 1)

                    x_step(h - 1, CHUNKS - 1)

                    @pl.when(h == hops)
                    def _():
                        work(h - 1, 1, n_pair)

                first, last = q * n_pair // CHUNKS, (q + 1) * n_pair // CHUNKS
                if last > first:
                    @pl.when(h < hops)
                    def _():
                        work(h - 1, first, last)
        return carry

    lax.fori_loop(0, hops + 1, stage, 0)

    embed = acc[...] * times
    unit = unit_ref[...]
    along = jnp.sum(unit * embed, 1, keepdims=True)
    grad_proj = ((embed - unit * along) / magnitude).astype(BF)
    local = tn(sf_ref[...], grad_proj)
    for k in range(tiles):
        part[k] = local[:, k * LANES : (k + 1) * LANES]

    here = pl.ds(pl.multiple_of(s * half, STAT_ROWS), half)
    there = pl.ds(pl.multiple_of((1 - s) * half, STAT_ROWS), half)
    half_out[...] = part[:, there, :].astype(BF)
    swap = pltpu.make_async_remote_copy(
        src_ref=half_out, dst_ref=half_in, send_sem=half_send.at[0], recv_sem=half_recv.at[0],
        device_id={"sub": 1 - s}, device_id_type=MESH,
    )
    swap.start()
    sg_ref[...] = nt(grad_proj, hw_ref[...]).astype(BF)
    swap.wait()
    part[:, here, :] = part[:, here, :] + half_in[...].astype(F32)
    mine[...] = part[:, here, :].astype(BF)

    def piece_of(index):
        return lax.rem(index, tiles), index // tiles * piece

    def c_copy(owner, source):
        tile_at, row_at = piece_of(owner)
        return pltpu.make_async_remote_copy(
            src_ref=mine.at[tile_at, pl.ds(pl.multiple_of(row_at, STAT_ROWS), piece)],
            dst_ref=chunks.at[source],
            send_sem=c_send.at[owner], recv_sem=c_recv.at[source],
            device_id=at_chip(owner), device_id_type=MESH,
        )

    def b_copy(other, source):
        return pltpu.make_async_remote_copy(
            src_ref=sums.at[s, source], dst_ref=sums.at[s, source],
            send_sem=b_send.at[other], recv_sem=b_recv.at[s, source],
            device_id=at_chip(other), device_id_type=MESH,
        )

    def f_copy(source, core):
        return pltpu.make_async_remote_copy(
            src_ref=sums.at[core, source], dst_ref=sums.at[core, source],
            send_sem=f_send.at[source], recv_sem=b_recv.at[core, source],
            device_id={"sub": 1 - s}, device_id_type=MESH,
        )

    def scatter(owner):
        @owns(owner)
        def _():
            c_copy(owner, chip).start()

    others(scatter)

    @owns(chip)
    def _():
        tile_at, row_at = piece_of(chip)
        first = part[tile_at, pl.ds(pl.multiple_of(s * half + row_at, STAT_ROWS), piece), :]

        def add(k, total):
            source = lax.rem(chip + k, chips)
            c_copy(chip, source).wait_recv()
            return total + chunks[source].astype(F32)

        sums[s, chip] = lax.fori_loop(1, chips, add, first).astype(BF)
        others(lambda other: b_copy(other, chip).start())
        f_copy(chip, s).start()

    def pass_on(source):
        @owns(source)
        def _():
            b_copy(source, source).wait_recv()
            f_copy(source, s).start()

    others(pass_on)

    def place_piece(core, source):
        tile_at, row_at = source % tiles, source // tiles * piece
        head_ref[
            core * half + row_at : core * half + row_at + piece,
            tile_at * LANES : (tile_at + 1) * LANES,
        ] = sums[core, source]

    for source in range(owners):
        f_copy(source, 1 - s).wait_recv()
    for source in range(owners):
        for core in range(2):
            place_piece(core, source)

    def left(other):
        @owns(other)
        def _():
            c_copy(other, chip).wait_send()

        @owns(chip)
        def _():
            b_copy(other, chip).wait_send()

    others(left)
    for source in range(owners):
        f_copy(source, s).wait_send()

    for d in range(2):
        @when(b + 1 - 2 * d)
        def _():
            for q in range(CHUNKS):
                z_copy(d, 0, q, own.at[q]).wait_send()
        for h in range(hops):
            @when(source_of(d, h))
            def _():
                for q in range(CHUNKS):
                    if h < hops - 1:
                        @when(b + 1 - 2 * d)
                        def _():
                            z_copy(d, h + 1, q, buf.at[d, h, p, s, q]).wait_send()
                    for k in range(1, n_pair):
                        x_copy(d, h, q, k).wait_send()
                    for k in range(n_pair):
                        s_copy(d, h, q, lax.rem(p + k, n_pair)).wait_send()


def solution(mesh):
    n_batch, n_pair = mesh.shape["batch"], mesh.shape["pair"]
    hops = min(ROUNDS, n_batch - 1)

    def body(teacher_feats, student_feats, head_weight, teacher_lse, student_lse):
        rows, wide = teacher_feats.shape
        sdim, edim = head_weight.shape
        depth = (wide + sdim) // LANES * (rows // CHUNKS) + STAT_ROWS
        chips, tiles, half = n_batch * n_pair, edim // LANES, sdim // 2
        piece = min(
            size for size in range(STAT_ROWS, half + 1, STAT_ROWS)
            if half % size == 0 and half // size * tiles <= chips
        )
        owners = half // piece * tiles
        vmem = pl.BlockSpec(memory_space=pltpu.VMEM)
        student_grad, head_sum = pl.pallas_call(
            functools.partial(kernel, n_batch, n_pair),
            out_shape=(
                jax.ShapeDtypeStruct((rows, sdim), BF),
                jax.ShapeDtypeStruct((sdim, edim), BF),
            ),
            in_specs=[vmem] * 5,
            out_specs=(vmem, vmem),
            scratch_shapes=[
                pltpu.VMEM((CHUNKS, depth, LANES), BF),
                pltpu.VMEM((2, hops, n_pair, 2, CHUNKS, depth, LANES), BF),
                pltpu.VMEM((rows, wide), BF),
                pltpu.VMEM((rows, edim), BF),
                pltpu.VMEM((rows, edim), F32),
                pltpu.VMEM((rows, edim), F32),
                pltpu.VMEM((tiles, sdim, LANES), F32),
                pltpu.VMEM((tiles, half, LANES), BF),
                pltpu.VMEM((tiles, half, LANES), BF),
                pltpu.VMEM((tiles, half, LANES), BF),
                pltpu.VMEM((chips, piece, LANES), BF),
                pltpu.VMEM((2, owners, piece, LANES), BF),
                pltpu.SemaphoreType.DMA((2, hops, CHUNKS)),
                pltpu.SemaphoreType.DMA((2, hops, n_pair, CHUNKS)),
                pltpu.SemaphoreType.DMA((2, hops, n_pair, CHUNKS)),
                pltpu.SemaphoreType.DMA((2, hops, n_pair, 2, CHUNKS)),
                pltpu.SemaphoreType.DMA((1,)),
                pltpu.SemaphoreType.DMA((1,)),
                pltpu.SemaphoreType.DMA((chips,)),
                pltpu.SemaphoreType.DMA((chips,)),
                pltpu.SemaphoreType.DMA((chips,)),
                pltpu.SemaphoreType.DMA((2, owners)),
                pltpu.SemaphoreType.DMA((owners,)),
            ],
            compiler_params=pltpu.CompilerParams(
                collective_id=0, has_side_effects=True, vmem_limit_bytes=56 * 1024 * 1024
            ),
        )(
            teacher_feats, student_feats, head_weight,
            teacher_lse.reshape(1, rows), student_lse.reshape(1, rows),
        )
        head_grad = head_sum.astype(F32) * HEAD_SCALE
        return student_grad, head_grad

    in_specs = (
        P(("groups", "batch", "pair", "sub"), None),
        P(("groups", "batch", "pair", "sub"), None),
        P(),
        P(("groups", "batch", "pair", "sub")),
        P(("groups", "batch", "pair", "sub")),
    )
    out_specs = (P(("groups", "batch", "pair", "sub"), None), P("groups", None))
    return jax.shard_map(body, mesh=mesh, in_specs=in_specs, out_specs=out_specs, check_vma=False)
```

```python
import functools

import jax
import jax.numpy as jnp
from jax import lax
from jax.experimental import pallas as pl
from jax.experimental.pallas import tpu as pltpu
from jax.sharding import PartitionSpec as P

TEACHER_TEMP = 0.04
STUDENT_TEMP = 0.05
LOSS_WEIGHT = 0.5
HEAD_SCALE = 0.0078125
EPSILON = 1e-06
ROUNDS = 3
LANES = 128
CHUNKS = 2
STAT_ROWS = 16
SWAPS = 2
MESH = pl.DeviceIdType.MESH
BF = jnp.bfloat16
F32 = jnp.float32


def nt(a, b):
    return lax.dot_general(a, b, (((1,), (1,)), ((), ())), preferred_element_type=F32)


def tn(a, b):
    return lax.dot_general(a, b, (((0,), (0,)), ((), ())), preferred_element_type=F32)


def project(feats, head):
    projected = jnp.dot(feats, head, preferred_element_type=F32)
    magnitude = jnp.sqrt(jnp.sum(projected * projected, 1, keepdims=True) + EPSILON)
    return projected / magnitude, magnitude


def kernel(
    n_batch, n_pair, tf_ref, sf_ref, hw_ref, tl_ref, sl_ref, sg_ref, head_ref,
    own, buf, t_own, u_own, unit_ref, acc, part, half_out, half_in, mine, chunks, sums,
    z_send, x_send, s_send, recv,
    half_send, half_recv, c_send, c_recv, b_send, b_recv, f_send,
):
    rows, wide = tf_ref.shape
    sdim = sf_ref.shape[1]
    per = rows // CHUNKS
    t_tiles, s_tiles = wide // LANES, sdim // LANES
    stat_at = (t_tiles + s_tiles) * per
    hops = min(ROUNDS, n_batch - 1)
    ring = n_batch > 2 * ROUNDS
    times = 1.0 if ring else 2.0
    b, p, s = lax.axis_index("batch"), lax.axis_index("pair"), lax.axis_index("sub")

    def place(index):
        return lax.rem(index + n_batch, n_batch) if ring else index

    def when(index):
        if ring:
            return lambda f: f()
        return pl.when(jnp.logical_and(index >= 0, index < n_batch))

    chips = n_batch * n_pair
    chip = b * n_pair + p
    tiles, half, _ = half_out.shape
    piece = chunks.shape[1]
    owners = sums.shape[1]

    def at_chip(index):
        return {"batch": index // n_pair, "pair": lax.rem(index, n_pair)}

    def owns(index):
        return pl.when(index < owners) if owners < chips else lambda f: f()

    def others(f):
        def one(k, carry):
            f(lax.rem(chip + k, chips))
            return carry

        lax.fori_loop(1, chips, one, 0)

    barrier = pltpu.get_barrier_semaphore()

    def greet(other):
        pl.semaphore_signal(barrier, inc=1, device_id=at_chip(other), device_id_type=MESH)

    others(greet)
    pl.semaphore_signal(barrier, inc=1, device_id={"sub": 1 - s}, device_id_type=MESH)

    wide_t = tf_ref[...].astype(F32)
    teacher = (
        wide_t / jnp.sqrt(jnp.sum(wide_t * wide_t, 1, keepdims=True) + EPSILON)
    ).astype(BF)
    t_own[...] = teacher
    stat_t, stat_s = jnp.exp(-tl_ref[...]), jnp.exp(-sl_ref[...])
    stat = jnp.concatenate([stat_t, stat_s, jnp.zeros((6, LANES), F32)], 0)
    high = stat.astype(BF)
    low = (stat - high.astype(F32)).astype(BF)
    stats = jnp.concatenate([high, low], 0)
    for q in range(CHUNKS):
        for k in range(t_tiles):
            own[q, k * per : (k + 1) * per, :] = teacher[
                q * per : (q + 1) * per, k * LANES : (k + 1) * LANES
            ]
        for k in range(s_tiles):
            at = (t_tiles + k) * per
            own[q, at : at + per, :] = sf_ref[
                q * per : (q + 1) * per, k * LANES : (k + 1) * LANES
            ]
        own[q, stat_at : stat_at + STAT_ROWS, :] = stats

    pl.semaphore_wait(barrier, chips)

    def z_copy(d, h, q, src):
        return pltpu.make_async_remote_copy(
            src_ref=src,
            dst_ref=buf.at[d, h, p, s, q],
            send_sem=z_send.at[d, h, q],
            recv_sem=recv.at[d, h, p, s, q],
            device_id={"batch": place(b + 1 - 2 * d)},
            device_id_type=MESH,
        )

    def x_copy(d, h, q, k):
        return pltpu.make_async_remote_copy(
            src_ref=buf.at[d, h, p, s, q],
            dst_ref=buf.at[d, h, p, s, q],
            send_sem=x_send.at[d, h, k, q],
            recv_sem=recv.at[d, h, p, s, q],
            device_id={"pair": lax.rem(p + k, n_pair)},
            device_id_type=MESH,
        )

    def s_copy(d, h, q, source):
        return pltpu.make_async_remote_copy(
            src_ref=buf.at[d, h, source, s, q],
            dst_ref=buf.at[d, h, source, s, q],
            send_sem=s_send.at[d, h, source, q],
            recv_sem=recv.at[d, h, source, s, q],
            device_id={"sub": 1 - s},
            device_id_type=MESH,
        )

    def arrived(d, h, source, core, q):
        pltpu.make_async_remote_copy(
            src_ref=buf.at[d, h, source, core, q],
            dst_ref=buf.at[d, h, source, core, q],
            send_sem=s_send.at[d, h, source, q],
            recv_sem=recv.at[d, h, source, core, q],
            device_id={"sub": 1 - s},
            device_id_type=MESH,
        ).wait_recv()

    for q in range(CHUNKS):
        for d in range(2):
            @when(b + 1 - 2 * d)
            def _():
                z_copy(d, 0, q, own.at[q]).start()

    unit, magnitude = project(sf_ref[...], hw_ref[...])
    unit_ref[...] = unit
    u_own[...] = unit.astype(BF)
    acc[...] = jnp.zeros_like(acc)
    tall = stat.T
    row_t, row_s = tall[:, 0:1], tall[:, 1:2]

    def source_of(d, h):
        return b - (1 - 2 * d) * (h + 1)

    def z_step(h, q):
        def each(d, carry):
            @when(source_of(d, h))
            def _():
                arrived(d, h, p, s, q)

                @pl.when(h < hops - 1)
                def _():
                    @when(b + 1 - 2 * d)
                    def _():
                        z_copy(d, h + 1, q, buf.at[d, h, p, s, q]).start()

                for k in range(1, n_pair):
                    x_copy(d, h, q, k).start()
                s_copy(d, h, q, p).start()
            return carry

        lax.fori_loop(0, 2, each, 0)

    def x_step(h, q):
        def each(d, carry):
            @when(source_of(d, h))
            def _():
                for k in range(1, n_pair):
                    source = lax.rem(p + k, n_pair)
                    arrived(d, h, source, s, q)
                    s_copy(d, h, q, source).start()
            return carry

        lax.fori_loop(0, 2, each, 0)

    def tile(d, h, source):
        for q in range(CHUNKS):
            arrived(d, h, source, 1 - s, q)
        t_parts, f_parts, st = [], [], []
        for core in range(2):
            for q in range(CHUNKS):
                t_parts.append(jnp.concatenate(
                    [buf[d, h, source, core, q, k * per : (k + 1) * per, :] for k in range(t_tiles)], 1
                ))
                f_parts.append(jnp.concatenate(
                    [
                        buf[d, h, source, core, q, (t_tiles + k) * per : (t_tiles + k + 1) * per, :]
                        for k in range(s_tiles)
                    ], 1
                ))
            raw = buf[d, h, source, core, 0, stat_at : stat_at + STAT_ROWS, :].astype(F32)
            st.append(raw[0:8] + raw[8:16])
        cols_t = jnp.concatenate(t_parts, 0)
        cols_f = jnp.concatenate(f_parts, 0)
        cols_s = jnp.concatenate(st, 1)
        cols_u = project(cols_f, hw_ref[...])[0].astype(BF)
        zt = nt(t_own[...], cols_t) * (1.0 / TEACHER_TEMP)
        zs = nt(u_own[...], cols_u) * (1.0 / STUDENT_TEMP)
        g = jnp.exp(zs) * (row_s + cols_s[1:2]) - jnp.exp(zt) * (row_t + cols_s[0:1])
        weights = (g * (LOSS_WEIGHT / STUDENT_TEMP)).astype(BF)
        acc[...] += jnp.dot(weights, cols_u, preferred_element_type=F32)

    def work(h, first, last):
        def each(d, carry):
            @when(source_of(d, h))
            def _():
                def one(k, c):
                    tile(d, h, lax.rem(p + k, n_pair))
                    return c

                lax.fori_loop(first, last, one, 0)
            return carry

        lax.fori_loop(0, 2, each, 0)

    def stage(h, carry):
        for q in range(CHUNKS):
            @pl.when(h < hops)
            def _():
                z_step(h, q)

            if q > 0:
                @pl.when(h < hops)
                def _():
                    x_step(h, q - 1)

            @pl.when(h > 0)
            def _():
                if q == 0:
                    @pl.when(h == hops)
                    def _():
                        work(h - 1, 0, 1)

                    x_step(h - 1, CHUNKS - 1)

                    @pl.when(h == hops)
                    def _():
                        work(h - 1, 1, n_pair)

                first, last = q * n_pair // CHUNKS, (q + 1) * n_pair // CHUNKS
                if last > first:
                    @pl.when(h < hops)
                    def _():
                        work(h - 1, first, last)
        return carry

    lax.fori_loop(0, hops + 1, stage, 0)

    embed = acc[...] * times
    unit = unit_ref[...]
    along = jnp.sum(unit * embed, 1, keepdims=True)
    grad_proj = ((embed - unit * along) / magnitude).astype(BF)
    local = tn(sf_ref[...], grad_proj)
    for k in range(tiles):
        part[k] = local[:, k * LANES : (k + 1) * LANES]

    here = pl.ds(pl.multiple_of(s * half, STAT_ROWS), half)
    there = pl.ds(pl.multiple_of((1 - s) * half, STAT_ROWS), half)
    groups = half_send.shape[0]
    share = tiles // groups

    def swap(i):
        at = pl.ds(i * share, share)
        return pltpu.make_async_remote_copy(
            src_ref=half_out.at[at], dst_ref=half_in.at[at],
            send_sem=half_send.at[i], recv_sem=half_recv.at[i],
            device_id={"sub": 1 - s}, device_id_type=MESH,
        )

    for i in range(groups):
        at = slice(i * share, (i + 1) * share)
        half_out[at] = part[at, there, :].astype(BF)
        swap(i).start()
    sg_ref[...] = nt(grad_proj, hw_ref[...]).astype(BF)

    def piece_of(index):
        return lax.rem(index, tiles), index // tiles * piece

    def c_copy(owner, source):
        tile_at, row_at = piece_of(owner)
        return pltpu.make_async_remote_copy(
            src_ref=mine.at[tile_at, pl.ds(pl.multiple_of(row_at, STAT_ROWS), piece)],
            dst_ref=chunks.at[source],
            send_sem=c_send.at[owner], recv_sem=c_recv.at[source],
            device_id=at_chip(owner), device_id_type=MESH,
        )

    def b_copy(other, source):
        return pltpu.make_async_remote_copy(
            src_ref=sums.at[s, source], dst_ref=sums.at[s, source],
            send_sem=b_send.at[other], recv_sem=b_recv.at[s, source],
            device_id=at_chip(other), device_id_type=MESH,
        )

    def f_copy(source, core):
        return pltpu.make_async_remote_copy(
            src_ref=sums.at[core, source], dst_ref=sums.at[core, source],
            send_sem=f_send.at[source], recv_sem=b_recv.at[core, source],
            device_id={"sub": 1 - s}, device_id_type=MESH,
        )

    def scatter(owner):
        @owns(owner)
        def _():
            c_copy(owner, chip).start()

    for i in range(groups):
        at = slice(i * share, (i + 1) * share)
        swap(i).wait()
        part[at, here, :] = part[at, here, :] + half_in[at].astype(F32)
        mine[at] = part[at, here, :].astype(BF)

        def scatter_part(other):
            tile_at = lax.rem(other, tiles)

            @pl.when(jnp.logical_and(tile_at >= i * share, tile_at < (i + 1) * share))
            def _():
                scatter(other)

        others(scatter_part)

    @owns(chip)
    def _():
        tile_at, row_at = piece_of(chip)
        first = part[tile_at, pl.ds(pl.multiple_of(s * half + row_at, STAT_ROWS), piece), :]

        def add(k, total):
            source = lax.rem(chip + chips - k, chips)
            c_copy(chip, source).wait_recv()
            return total + chunks[source].astype(F32)

        sums[s, chip] = lax.fori_loop(1, chips, add, first).astype(BF)
        others(lambda other: b_copy(other, chip).start())
        f_copy(chip, s).start()

    def pass_on(source):
        @owns(source)
        def _():
            b_copy(source, source).wait_recv()
            f_copy(source, s).start()

    def in_order(k, carry):
        pass_on(lax.rem(chip + chips - k, chips))
        return carry

    lax.fori_loop(1, chips, in_order, 0)

    def place_piece(core, source):
        tile_at, row_at = source % tiles, source // tiles * piece
        head_ref[
            core * half + row_at : core * half + row_at + piece,
            tile_at * LANES : (tile_at + 1) * LANES,
        ] = sums[core, source]

    for source in range(owners):
        f_copy(source, 1 - s).wait_recv()
    for source in range(owners):
        for core in range(2):
            place_piece(core, source)

    def left(other):
        @owns(other)
        def _():
            c_copy(other, chip).wait_send()

        @owns(chip)
        def _():
            b_copy(other, chip).wait_send()

    others(left)
    for source in range(owners):
        f_copy(source, s).wait_send()

    for d in range(2):
        @when(b + 1 - 2 * d)
        def _():
            for q in range(CHUNKS):
                z_copy(d, 0, q, own.at[q]).wait_send()
        for h in range(hops):
            @when(source_of(d, h))
            def _():
                for q in range(CHUNKS):
                    if h < hops - 1:
                        @when(b + 1 - 2 * d)
                        def _():
                            z_copy(d, h + 1, q, buf.at[d, h, p, s, q]).wait_send()
                    for k in range(1, n_pair):
                        x_copy(d, h, q, k).wait_send()
                    for k in range(n_pair):
                        s_copy(d, h, q, lax.rem(p + k, n_pair)).wait_send()


def solution(mesh):
    n_batch, n_pair = mesh.shape["batch"], mesh.shape["pair"]
    hops = min(ROUNDS, n_batch - 1)

    def body(teacher_feats, student_feats, head_weight, teacher_lse, student_lse):
        rows, wide = teacher_feats.shape
        sdim, edim = head_weight.shape
        depth = (wide + sdim) // LANES * (rows // CHUNKS) + STAT_ROWS
        chips, tiles, half = n_batch * n_pair, edim // LANES, sdim // 2
        piece = min(
            size for size in range(STAT_ROWS, half + 1, STAT_ROWS)
            if half % size == 0 and half // size * tiles <= chips
        )
        owners = half // piece * tiles
        vmem = pl.BlockSpec(memory_space=pltpu.VMEM)
        student_grad, head_sum = pl.pallas_call(
            functools.partial(kernel, n_batch, n_pair),
            out_shape=(
                jax.ShapeDtypeStruct((rows, sdim), BF),
                jax.ShapeDtypeStruct((sdim, edim), BF),
            ),
            in_specs=[vmem] * 5,
            out_specs=(vmem, vmem),
            scratch_shapes=[
                pltpu.VMEM((CHUNKS, depth, LANES), BF),
                pltpu.VMEM((2, hops, n_pair, 2, CHUNKS, depth, LANES), BF),
                pltpu.VMEM((rows, wide), BF),
                pltpu.VMEM((rows, edim), BF),
                pltpu.VMEM((rows, edim), F32),
                pltpu.VMEM((rows, edim), F32),
                pltpu.VMEM((tiles, sdim, LANES), F32),
                pltpu.VMEM((tiles, half, LANES), BF),
                pltpu.VMEM((tiles, half, LANES), BF),
                pltpu.VMEM((tiles, half, LANES), BF),
                pltpu.VMEM((chips, piece, LANES), BF),
                pltpu.VMEM((2, owners, piece, LANES), BF),
                pltpu.SemaphoreType.DMA((2, hops, CHUNKS)),
                pltpu.SemaphoreType.DMA((2, hops, n_pair, CHUNKS)),
                pltpu.SemaphoreType.DMA((2, hops, n_pair, CHUNKS)),
                pltpu.SemaphoreType.DMA((2, hops, n_pair, 2, CHUNKS)),
                pltpu.SemaphoreType.DMA((SWAPS,)),
                pltpu.SemaphoreType.DMA((SWAPS,)),
                pltpu.SemaphoreType.DMA((chips,)),
                pltpu.SemaphoreType.DMA((chips,)),
                pltpu.SemaphoreType.DMA((chips,)),
                pltpu.SemaphoreType.DMA((2, owners)),
                pltpu.SemaphoreType.DMA((owners,)),
            ],
            compiler_params=pltpu.CompilerParams(
                collective_id=0, has_side_effects=True, vmem_limit_bytes=56 * 1024 * 1024
            ),
        )(
            teacher_feats, student_feats, head_weight,
            teacher_lse.reshape(1, rows), student_lse.reshape(1, rows),
        )
        head_grad = head_sum.astype(F32) * HEAD_SCALE
        return student_grad, head_grad

    in_specs = (
        P(("groups", "batch", "pair", "sub"), None),
        P(("groups", "batch", "pair", "sub"), None),
        P(),
        P(("groups", "batch", "pair", "sub")),
        P(("groups", "batch", "pair", "sub")),
    )
    out_specs = (P(("groups", "batch", "pair", "sub"), None), P("groups", None))
    return jax.shard_map(body, mesh=mesh, in_specs=in_specs, out_specs=out_specs, check_vma=False)
```
